32 devices in a mesh: dp: 16 (over z, x, core), tensor: 2 (over y).
Axes of the slice: x: 2, y: 2, z: 4, core: 2. Of those that a mesh axis runs over, the one named last changes fastest.
Arguments:
- tokens: bfloat16 [16384, 1024], P(('dp', 'tensor')), may hold values from -6 to 6
- ln1_gain: float32 [1024], replicated, may hold values from 0.5 to 1.5
- ln1_bias: float32 [1024], replicated, may hold values from -1.75 to 1.75
- w_qkv: bfloat16 [3, 1024, 1024], P(None, 'dp', 'tensor'), may hold values from -0.25 to 0.25
- qv_bias: float32 [2, 1024], replicated, may hold values from -3 to 3
- w_out: bfloat16 [1024, 1024], P('tensor', 'dp'), may hold values from -0.75 to 0.75
- out_bias: float32 [1024], replicated, may hold values from -1.75 to 1.75
- ln2_gain: float32 [1024], replicated, may hold values from 0.5 to 1.5
- ln2_bias: float32 [1024], replicated, may hold values from -1.75 to 1.75
- w_fc: bfloat16 [1024, 4096], P('dp', 'tensor'), may hold values from -0.1875 to 0.1875
- fc_bias: float32 [4096], replicated, may hold values from -3 to 3
- w_proj: bfloat16 [4096, 1024], P('tensor', 'dp'), may hold values from -0.125 to 0.125
- proj_bias: float32 [1024], replicated, may hold values from -1.75 to 1.75
- cotangent: bfloat16 [16384, 1024], P(('dp', 'tensor')), may hold values from -6 to 6
Outputs:
- block_out: bfloat16 [16384, 1024], P(('dp', 'tensor'))
- input_grad: bfloat16 [16384, 1024], P(('dp', 'tensor'))
- grad_ln1_gain: float32 [1024], replicated
- grad_ln1_bias: float32 [1024], replicated
- grad_qkv: float32 [3, 1024, 1024], P(None, 'dp', 'tensor')
- grad_qv_bias: float32 [2, 1024], replicated
- grad_out: float32 [1024, 1024], P('tensor', 'dp')
- grad_out_bias: float32 [1024], replicated
- grad_ln2_gain: float32 [1024], replicated
- grad_ln2_bias: float32 [1024], replicated
- grad_fc: float32 [1024, 4096], P('dp', 'tensor')
- grad_fc_bias: float32 [4096], replicated
- grad_proj: float32 [4096, 1024], P('tensor', 'dp')
- grad_proj_bias: float32 [1024], replicated
The draws below stay inside these ranges and needn't reach their ends.
All inputs are finite; a program needn't handle non-finite values.
Results may differ from the reference program's by a relative error of at most 0.018.
Values may be sent and summed in bfloat16 or wider, within the bound.
A program may use at most 192 MiB of HBM per device.

```python
import math
import jax
import jax.numpy as jnp
from jax import lax

D = 1024
H = 16
HD = 64
FF = 4096
LEN = 1024
QBLK = 512
GROUP = 1024
TOKENS = 16384
N_DP = 16


def spiked(values, own_key, source, target, blocks, factor):
    owner, partner = [(jnp.arange(values.shape[position]) // (values.shape[position] // blocks)).reshape([-1 if axis == position else 1 for axis in range(values.ndim)]) for position in (source, target)]
    chosen = jax.random.permutation(own_key, blocks)[partner]
    strong = (owner == chosen) | (owner == (partner + blocks // 2) % blocks)
    return jnp.where(strong, factor * values, values)


def shard_levels(key, dims, shards, low, largest):
    level, own = 1.0, jax.random.fold_in(key, 6)
    for dim, shards_of in shards:
        heights = jnp.exp(jax.random.uniform(jax.random.fold_in(own, dim), (shards_of,), jnp.float32, low / len(shards), largest / len(shards)))
        level = level * jnp.repeat(heights, dims[dim] // shards_of).reshape([-1 if axis == dim else 1 for axis in range(len(dims))])
    return level


def noise(own_key, extent, scale, bound, cuts=(), kind=jnp.bfloat16):
    factor_of = shard_levels(own_key, extent, cuts, -0.22, 0.18) if cuts else 1.0
    drawn = jax.random.normal(own_key, extent, jnp.float32) * scale * factor_of
    return jnp.minimum(jnp.maximum(drawn, -bound), bound).astype(kind)


def bell_draw_with(stream_key, shape, width, reach, shards, heavy, held_as=jnp.bfloat16):
    values = width * jax.random.normal(stream_key, shape, jnp.float32)
    if shards:
        values = values * shard_levels(stream_key, shape, shards, -0.22, 0.18)
    return jnp.clip(spiked(values, jax.random.fold_in(stream_key, 3), *heavy), -reach, reach).astype(held_as)


def setup_inputs(seed: int = 0) -> dict:
    keys = jax.random.split(jax.random.key(seed), 15)
    return {
        "tokens": noise(keys[0], (TOKENS, D), 1.0, 6.0, ((0, 32),)),
        "ln1_gain": jnp.clip(1.0 + 0.1 * jax.random.normal(keys[1], (D,), jnp.float32), 0.5, 1.5),
        "ln1_bias": noise(keys[2], (D,), 0.3, 1.75, (), jnp.float32),
        "w_qkv": noise(keys[3], (3, D, D), (D // 2) ** -0.5, 0.25, ((1, 16), (2, 2))),
        "qv_bias": noise(keys[4], (2, D), 0.5, 3.0, (), jnp.float32),
        "w_out": noise(keys[5], (D, D), (D // 16) ** -0.5, 0.75, ((0, 2), (1, 16))),
        "out_bias": noise(keys[6], (D,), 0.3, 1.75, (), jnp.float32),
        "ln2_gain": jnp.clip(1.0 + 0.1 * jax.random.normal(keys[7], (D,), jnp.float32), 0.5, 1.5),
        "ln2_bias": noise(keys[8], (D,), 0.3, 1.75, (), jnp.float32),
        "w_fc": noise(keys[9], (D, FF), D ** -0.5, 0.1875, ((0, 16), (1, 2))),
        "fc_bias": noise(keys[10], (FF,), 0.5, 3.0, (), jnp.float32),
        "w_proj": noise(keys[11], (FF, D), (FF // 2) ** -0.5, 0.125, ((0, 2), (1, 16))),
        "proj_bias": noise(keys[12], (D,), 0.3, 1.75, (), jnp.float32),
        "cotangent": bell_draw_with(keys[13], (TOKENS, D), 1.0, 6.0, ((0, 32),), (0, 1, 32, 2.75)),
    }


EPSILON = 1e-05
HIGHEST = lax.Precision.HIGHEST

@jax.custom_vjp
def low(v):
    return lax.optimization_barrier(v.astype(jnp.bfloat16)).astype(jnp.float32)

@jax.custom_vjp
def low_back(v):
    return v

def low_keep(v):
    return (low(v), None)

def low_pass(kept, grad):
    return (grad,)

def back_keep(v):
    return (v, None)

def back_low(kept, grad):
    return (low(grad),)
low.defvjp(low_keep, low_pass)
low_back.defvjp(back_keep, back_low)

def norm_rows(rows_in, gain, shift):
    centre = lax.optimization_barrier(jnp.mean(rows_in, axis=-1, keepdims=True))
    centred = rows_in - centre
    spread = lax.optimization_barrier(jnp.mean(centred * centred, axis=-1, keepdims=True))
    return centred * lax.rsqrt(spread + EPSILON) * gain + shift

def both_ways(matrix):
    return low(low_back(matrix))

def product(left_side, right_side):
    return jnp.dot(left_side, right_side, precision=HIGHEST, preferred_element_type=jnp.float32)

def attend_block(query_block, key_seq, value_seq, block_start):
    scores = jnp.einsum('qhd,khd->hqk', query_block, key_seq, precision=HIGHEST) * (1.0 / math.sqrt(HD))
    scores = low_back(scores)
    query_pos = block_start + lax.broadcasted_iota(jnp.int32, (QBLK, LEN), 0)
    key_pos = lax.broadcasted_iota(jnp.int32, (QBLK, LEN), 1)
    scores = jnp.where((key_pos <= query_pos)[None], scores, -1e+30)
    row_top = lax.optimization_barrier(jnp.max(scores, axis=-1, keepdims=True))
    weights = jnp.exp(scores - row_top)
    probabilities = weights / lax.optimization_barrier(jnp.sum(weights, axis=-1, keepdims=True))
    return jnp.einsum('hqk,khd->qhd', low(probabilities), value_seq, precision=HIGHEST)
attend_step = jax.checkpoint(attend_block)

def block_forward(inputs, ln1_gain, ln1_bias, w_qkv, qv_bias, w_out, out_bias, ln2_gain, ln2_bias, w_fc, fc_bias, w_proj, proj_bias):
    row_count = inputs.shape[0]
    seq_count = row_count // LEN
    per_seq = LEN // QBLK
    normed = low(norm_rows(inputs, ln1_gain, ln1_bias))
    queries = both_ways(product(normed, w_qkv[0]) + qv_bias[0])
    key_rows = both_ways(product(normed, w_qkv[1]))
    value_rows = both_ways(product(normed, w_qkv[2]) + qv_bias[1])
    query_blocks = queries.reshape(seq_count, per_seq, QBLK, H, HD)
    key_seqs = key_rows.reshape(seq_count, LEN, H, HD)
    value_seqs = value_rows.reshape(seq_count, LEN, H, HD)

    def per_sequence(triple):
        query_seq, key_seq, value_seq = triple

        def per_block(couple):
            query_block, block_index = couple
            return attend_step(query_block, key_seq, value_seq, block_index * QBLK)
        return lax.map(per_block, (query_seq, jnp.arange(per_seq, dtype=jnp.int32)))
    attended = lax.map(per_sequence, (query_blocks, key_seqs, value_seqs)).reshape(row_count, D)
    attended = both_ways(attended)
    hidden = inputs + low_back(product(attended, w_out) + out_bias)
    normed_two = low(norm_rows(hidden, ln2_gain, ln2_bias))
    pre_act = low_back(product(normed_two, w_fc) + fc_bias)
    activated = low(jax.nn.gelu(pre_act, approximate=True))
    return hidden + low_back(product(activated, w_proj) + proj_bias)

def reference(tokens, ln1_gain, ln1_bias, w_qkv, qv_bias, w_out, out_bias, ln2_gain, ln2_bias, w_fc, fc_bias, w_proj, proj_bias, cotangent):
    params = tuple((element.astype(jnp.float32) for element in (ln1_gain, ln1_bias, w_qkv, qv_bias, w_out, out_bias, ln2_gain, ln2_bias, w_fc, fc_bias, w_proj, proj_bias)))
    inputs = tokens.astype(jnp.float32).reshape(N_DP, GROUP, D)
    grads_in = cotangent.astype(jnp.float32).reshape(N_DP, GROUP, D)

    def one_group(totals, group_pair):
        group_in, group_grad = group_pair
        result, pullback = jax.vjp(block_forward, group_in, *params)
        gradients = pullback(group_grad)
        totals = tuple((running + update for running, update in zip(totals, gradients[1:])))
        return (totals, (result.astype(jnp.bfloat16), gradients[0].astype(jnp.bfloat16)))
    initial = tuple((jnp.zeros_like(element) for element in params))
    totals, (outputs, input_grads) = lax.scan(one_group, initial, (inputs, grads_in))
    return (outputs.reshape(TOKENS, D), input_grads.reshape(TOKENS, D), totals[0], totals[1], totals[2], totals[3], totals[4], totals[5], totals[6], totals[7], totals[8], totals[9], totals[10], totals[11])
```

```python
import math

import jax
import jax.numpy as jnp
from jax import lax
from jax.experimental import pallas as pl
from jax.experimental.pallas import tpu as pltpu
from jax.sharding import PartitionSpec as P

HD = 64
LEN = 1024
QB = 256
LANES = 128


EPSILON = 1e-05


def norm_rows(rows_in, gain, shift):
    centre = jnp.mean(rows_in, axis=-1, keepdims=True)
    centred = rows_in - centre
    spread = jnp.mean(centred * centred, axis=-1, keepdims=True)
    return centred * lax.rsqrt(spread + EPSILON) * gain + shift


def gelu_tanh(pre_act):
    return jax.nn.gelu(pre_act, approximate=True)


def shift_by(values, step):
    size = lax.axis_size("tensor")
    return lax.ppermute(values, "tensor", [(i, (i + step) % size) for i in range(size)])


def gather_rows(local_rows):
    size = lax.axis_size("tensor")
    rank = lax.axis_index("tensor")
    rows = local_rows.shape[0]
    pieces = [shift_by(local_rows, step) for step in range(1, size)]
    if size == 2:
        first = jnp.where(rank == 0, local_rows, pieces[0])
        second = jnp.where(rank == 0, pieces[0], local_rows)
        return jnp.concatenate([first, second], axis=0)
    whole = jnp.zeros((rows * size,) + local_rows.shape[1:], local_rows.dtype)
    whole = lax.dynamic_update_slice_in_dim(whole, local_rows, rank * rows, 0)
    for step, piece in enumerate(pieces, 1):
        whole = lax.dynamic_update_slice_in_dim(whole, piece, (rank - step) % size * rows, 0)
    return whole


def spread_product(left_side, product, rows):
    size = lax.axis_size("tensor")
    rank = lax.axis_index("tensor")

    def piece_for(owner):
        return product(lax.dynamic_slice_in_dim(left_side, owner * rows, rows, 0))

    arrived = [
        shift_by(piece_for((rank + step) % size).astype(jnp.bfloat16), step)
        for step in range(1, size)
    ]
    total = piece_for(rank)
    for piece in arrived:
        total = total + piece.astype(jnp.float32)
    return total


def sum_everywhere(vectors):
    sizes = [v.size for v in vectors]
    flat = jnp.concatenate([v.reshape(-1) for v in vectors]).reshape(-1, LANES)
    for axis in ("tensor", "dp"):
        size = lax.axis_size(axis)
        hop = 1
        while hop < size:
            flat = flat + lax.ppermute(flat, axis, [(i, i ^ hop) for i in range(size)])
            hop *= 2
    flat = flat.reshape(-1)
    out, start = [], 0
    for v, n in zip(vectors, sizes):
        out.append(flat[start : start + n].reshape(v.shape))
        start += n
    return out


def contract_rows(left_side, right_side):
    return lax.dot_general(
        left_side, right_side, (((0,), (0,)), ((), ())), preferred_element_type=jnp.float32
    )


def contract_cols(left_side, right_side):
    return lax.dot_general(
        left_side, right_side, (((1,), (1,)), ((), ())), preferred_element_type=jnp.float32
    )


def times(left_side, right_side):
    return jnp.dot(left_side, right_side, preferred_element_type=jnp.float32)


SCALE = 1.0 / math.sqrt(HD)


def only_head(values, head):
    lane = lax.broadcasted_iota(jnp.int32, values.shape, 1)
    return jnp.where(lane // HD == head, values, jnp.zeros_like(values))


def causal_scores(query_block, keys, start):
    scores = contract_cols(query_block, keys) * SCALE
    row = lax.broadcasted_iota(jnp.int32, scores.shape, 0) + start
    col = lax.broadcasted_iota(jnp.int32, scores.shape, 1)
    return jnp.where(col <= row, scores, -1e30)


def forward_kernel(q_ref, k_ref, v_ref, o_ref, lse_ref):
    keys = [only_head(k_ref[...], head) for head in range(2)]
    values = [only_head(v_ref[...], head) for head in range(2)]
    lane = lax.broadcasted_iota(jnp.int32, (QB, LANES), 1)
    for block in range(LEN // QB):
        start, stop = block * QB, (block + 1) * QB
        query_block = q_ref[start:stop, :]
        attended = jnp.zeros((QB, LANES), jnp.float32)
        logs = []
        for head in range(2):
            scores = causal_scores(query_block, keys[head][:stop], start)
            top = jnp.max(scores, axis=-1, keepdims=True)
            weights = jnp.exp(scores - top)
            total = jnp.sum(weights, axis=-1, keepdims=True)
            weights = (weights * (1.0 / total)).astype(jnp.bfloat16)
            attended += times(weights, values[head][:stop])
            logs.append(top + jnp.log(total))
        o_ref[start:stop, :] = attended.astype(jnp.bfloat16)
        lse_ref[start:stop, :] = jnp.where(lane < HD, logs[0], logs[1])


def backward_kernel(q_ref, k_ref, v_ref, o_ref, do_ref, lse_ref, out_ref, dk_ref, dv_ref):
    pair = pl.program_id(1)
    width = out_ref.shape[1] // 3
    keys = [only_head(k_ref[...], head) for head in range(2)]
    values = [only_head(v_ref[...], head) for head in range(2)]
    dk_ref[...] = jnp.zeros_like(dk_ref)
    dv_ref[...] = jnp.zeros_like(dv_ref)

    def columns(part):
        return pl.ds(pl.multiple_of(part * width + pair * LANES, LANES), LANES)

    for block in range(LEN // QB):
        start, stop = block * QB, (block + 1) * QB
        query_block = q_ref[start:stop, :]
        d_block = do_ref[start:stop, :]
        both = d_block.astype(jnp.float32) * o_ref[start:stop, :].astype(jnp.float32)
        d_query = jnp.zeros((QB, LANES), jnp.float32)
        for head in range(2):
            scores = causal_scores(query_block, keys[head][:stop], start)
            weights = jnp.exp(scores - lse_ref[start:stop, head * HD : head * HD + 1])
            d_weights = contract_cols(d_block, values[head][:stop])
            delta = jnp.sum(only_head(both, head), axis=-1, keepdims=True)
            d_scores = (weights * (d_weights - delta)).astype(jnp.bfloat16)
            d_query += times(d_scores, keys[head][:stop])
            dk_ref[:stop, :] += contract_rows(d_scores, only_head(query_block, head))
            dv_ref[:stop, :] += contract_rows(
                weights.astype(jnp.bfloat16), only_head(d_block, head)
            )
        out_ref[start:stop, columns(0)] = (d_query * SCALE).astype(jnp.bfloat16)
    out_ref[:, columns(1)] = (dk_ref[...] * SCALE).astype(jnp.bfloat16)
    out_ref[:, columns(2)] = dv_ref[...].astype(jnp.bfloat16)


def pair_block(part, pairs):
    return pl.BlockSpec((LEN, LANES), lambda s, p: (s, part * pairs + p))


def attend_forward(qkv):
    rows, width = qkv.shape[0], qkv.shape[1] // 3
    pairs = width // LANES
    return pl.pallas_call(
        forward_kernel,
        grid=(rows // LEN, pairs),
        in_specs=[pair_block(part, pairs) for part in range(3)],
        out_specs=[pair_block(0, pairs), pair_block(0, pairs)],
        out_shape=[
            jax.ShapeDtypeStruct((rows, width), jnp.bfloat16),
            jax.ShapeDtypeStruct((rows, width), jnp.float32),
        ],
        compiler_params=pltpu.CompilerParams(vmem_limit_bytes=40 * 2**20),
        cost_estimate=pl.CostEstimate(
            flops=8 * rows * LEN * width, bytes_accessed=10 * rows * width, transcendentals=0
        ),
        name="attend_forward",
    )(qkv, qkv, qkv)


def attend_backward(qkv, attended, d_attended, log_totals):
    rows, width = qkv.shape[0], qkv.shape[1] // 3
    pairs = width // LANES
    return pl.pallas_call(
        backward_kernel,
        grid=(rows // LEN, pairs),
        in_specs=[pair_block(part, pairs) for part in range(3)] + [pair_block(0, pairs)] * 3,
        out_specs=pl.BlockSpec((LEN, 3 * width), lambda s, p: (s, 0)),
        out_shape=jax.ShapeDtypeStruct((rows, 3 * width), jnp.bfloat16),
        scratch_shapes=[pltpu.VMEM((LEN, LANES), jnp.float32)] * 2,
        compiler_params=pltpu.CompilerParams(vmem_limit_bytes=40 * 2**20),
        cost_estimate=pl.CostEstimate(
            flops=20 * rows * LEN * width, bytes_accessed=20 * rows * width, transcendentals=0
        ),
        name="attend_backward",
    )(qkv, qkv, qkv, attended, d_attended, log_totals)


def over_dp(shard):
    return lax.all_gather(shard, "dp", axis=0, tiled=True)


def shard_over_dp(grad):
    return lax.psum_scatter(grad, "dp", scatter_dimension=0, tiled=True)


def body(
    tokens,
    ln1_gain,
    ln1_bias,
    w_qkv,
    qv_bias,
    w_out,
    out_bias,
    ln2_gain,
    ln2_bias,
    w_fc,
    fc_bias,
    w_proj,
    proj_bias,
    cotangent,
):
    tok_rows = tokens.shape[0]
    tensor_rank = lax.axis_index("tensor")
    head_cols = w_qkv.shape[2]
    hidden_cols = w_fc.shape[1]
    attn_shard = jnp.concatenate([w_qkv[0], w_qkv[1], w_qkv[2], w_out.T], axis=1)
    attn_full = over_dp(attn_shard)
    qkv_full = attn_full[:, : 3 * head_cols]
    out_cols = attn_full[:, 3 * head_cols :]
    fc_full = over_dp(w_fc)
    proj_full = over_dp(w_proj.T)

    bias_qv = lax.dynamic_slice_in_dim(qv_bias, tensor_rank * head_cols, head_cols, 1)
    bias_qkv = jnp.concatenate([bias_qv[0], jnp.zeros_like(bias_qv[0]), bias_qv[1]])
    inputs = tokens.astype(jnp.float32)
    normed_one, norm_one_back = jax.vjp(norm_rows, inputs, ln1_gain, ln1_bias)
    seen_one = gather_rows(normed_one.astype(jnp.bfloat16))
    seen_grad = gather_rows(cotangent)
    qkv = (times(seen_one, qkv_full) + bias_qkv).astype(jnp.bfloat16)
    attended, log_totals = attend_forward(qkv)
    branch_one = spread_product(attended, lambda piece: contract_cols(piece, out_cols), tok_rows)
    hidden_res = inputs + (branch_one + out_bias)
    normed_two, norm_two_back = jax.vjp(norm_rows, hidden_res, ln2_gain, ln2_bias)
    seen_two = gather_rows(normed_two.astype(jnp.bfloat16))
    bias_hidden = lax.dynamic_slice_in_dim(fc_bias, tensor_rank * hidden_cols, hidden_cols, 0)
    pre_act = times(seen_two, fc_full) + bias_hidden
    activated, gelu_back = jax.vjp(gelu_tanh, pre_act)
    activated = activated.astype(jnp.bfloat16)
    d_pre = gelu_back(times(seen_grad, proj_full))[0].astype(jnp.bfloat16)
    d_normed_two = spread_product(d_pre, lambda piece: contract_cols(piece, fc_full), tok_rows)
    grad_proj = shard_over_dp(contract_rows(seen_grad, activated).astype(jnp.bfloat16))
    branch_two = spread_product(activated, lambda piece: contract_cols(piece, proj_full), tok_rows)
    block_out = (hidden_res + (branch_two + proj_bias)).astype(jnp.bfloat16)
    grad_fc = shard_over_dp(contract_rows(seen_two, d_pre).astype(jnp.bfloat16))

    grad_final = cotangent.astype(jnp.float32)
    grad_proj_bias = jnp.sum(grad_final, axis=0)
    local_bias_grad = jnp.sum(d_pre, axis=0, dtype=jnp.float32)
    grad_fc_bias = lax.dynamic_update_slice_in_dim(
        jnp.zeros(fc_bias.shape, jnp.float32), local_bias_grad, tensor_rank * hidden_cols, 0
    )
    d_hidden_norm, grad_ln2_gain, grad_ln2_bias = norm_two_back(d_normed_two)
    grad_hidden = grad_final + d_hidden_norm
    grad_hidden_low = grad_hidden.astype(jnp.bfloat16)
    grad_out_bias = jnp.sum(grad_hidden_low, axis=0, dtype=jnp.float32)
    seen_hidden = gather_rows(grad_hidden_low)
    d_attended = times(seen_hidden, out_cols).astype(jnp.bfloat16)
    early = sum_everywhere(
        [grad_out_bias, grad_ln2_gain, grad_ln2_bias, grad_fc_bias, grad_proj_bias]
    )
    d_qkv_rows = attend_backward(qkv, attended, d_attended, log_totals)
    d_normed_one = spread_product(
        d_qkv_rows, lambda piece: contract_cols(piece, qkv_full), tok_rows
    )
    grad_attn = shard_over_dp(
        jnp.concatenate(
            [
                contract_rows(seen_one, d_qkv_rows).astype(jnp.bfloat16),
                contract_rows(seen_hidden, attended).astype(jnp.bfloat16),
            ],
            axis=1,
        )
    ).astype(jnp.float32)
    bias_sums = jnp.sum(d_qkv_rows, axis=0, dtype=jnp.float32)
    local_qv = jnp.stack([bias_sums[:head_cols], bias_sums[2 * head_cols :]])
    grad_qv_bias = lax.dynamic_update_slice_in_dim(
        jnp.zeros(qv_bias.shape, jnp.float32), local_qv, tensor_rank * head_cols, 1
    )
    d_inputs_norm, grad_ln1_gain, grad_ln1_bias = norm_one_back(d_normed_one)
    input_grad = (grad_hidden + d_inputs_norm).astype(jnp.bfloat16)
    late = sum_everywhere([grad_ln1_gain, grad_ln1_bias, grad_qv_bias])
    grad_qkv = jnp.stack(
        [grad_attn[:, part * head_cols : (part + 1) * head_cols] for part in range(3)]
    )
    return (
        block_out,
        input_grad,
        late[0],
        late[1],
        grad_qkv,
        late[2],
        grad_attn[:, 3 * head_cols :].T,
        early[0],
        early[1],
        early[2],
        grad_fc.astype(jnp.float32),
        early[3],
        grad_proj.astype(jnp.float32).T,
        early[4],
    )


def solution(mesh):
    in_specs = (
        P(("dp", "tensor"), None),
        P(),
        P(),
        P(None, "dp", "tensor"),
        P(),
        P("tensor", "dp"),
        P(),
        P(),
        P(),
        P("dp", "tensor"),
        P(),
        P("tensor", "dp"),
        P(),
        P(("dp", "tensor"), None),
    )
    out_specs = (
        P(("dp", "tensor"), None),
        P(("dp", "tensor"), None),
        P(),
        P(),
        P(None, "dp", "tensor"),
        P(),
        P("tensor", "dp"),
        P(),
        P(),
        P(),
        P("dp", "tensor"),
        P(),
        P("tensor", "dp"),
        P(),
    )
    return jax.shard_map(body, mesh=mesh, in_specs=in_specs, out_specs=out_specs, check_vma=False)
```
